32 devices in a mesh: grp: 4 (over y, x), hh: 8 (over z, core).
Axes of the slice: x: 2, y: 2, z: 4, core: 2. Of those that a mesh axis runs over, the one named last changes fastest.
Arguments:
- hh_factors: bfloat16 [8192, 256], P('hh')
- prod_init: float32 [6144, 256], P(('grp', 'hh')), may hold values from -1.2 to 1.2
- hh_index: int32 [4, 192, 8, 8, 8], P('grp', None, None, 'hh'), may hold values from 0 to 1023
- trips: int32 [4, 192, 8, 8, 8], P('grp', None, None, 'hh'), may hold values from 1 to 8
- counts: int32 [4, 192, 8, 8], P('grp', None, None, 'hh'), may hold values from 0 to 8, as said below
Outputs:
- prod_factors: float32 [6144, 256], P(('grp', 'hh'))
The draws below stay inside these ranges and needn't reach their ends.
Inputs may be any that keep to these rules, and one draw needn't show every extreme that they name: `hh_index`: a household row within its owner's shard. `counts`: live slots of one product from one source shard; 8 is reached in every draw.
All inputs are finite; a program needn't handle non-finite values.
Results may differ from the reference program's by a relative error of at most 0.0003.
The reference program's roundings to bfloat16 on the way (of `weighted` and `coef`) count: a program that leaves them out, or rounds other values in their place, can miss the bound.
Values may be sent and summed in bfloat16 or wider, within the bound.
A program may use at most 128 MiB of HBM per device.

```python
import jax
import jax.numpy as jnp
from jax import lax

K = 256
P_DEV = 192
HH_DEV = 1024
CAP = 8
P_SIZE = 6144
H = 8192
N_GRP = 4
N_HH = 8


def draw_hh_factors(key, part):
    key = jax.random.fold_in(key, 11)
    key_main, key_mean = jax.random.split(key, 2)
    column_means = jax.random.uniform(key_mean, (1, K), jnp.float32, -0.6, 0.6)
    base = jax.random.normal(key_main, (H, K), jnp.float32)
    return ((base + column_means) * K ** (-0.5)).astype(jnp.bfloat16)


def draw_counts(key, part):
    key = jax.random.fold_in(key, 5)
    key_level, key_base = jax.random.split(key, 2)
    level = jax.random.randint(key_level, (N_GRP, P_DEV, 1, 1), 1, 4)
    base = jax.random.randint(key_base, (N_GRP, P_DEV, N_HH, N_HH), 0, CAP // 2 + 1)
    filled = jnp.minimum(CAP, base * level)
    owner = lax.broadcasted_iota(jnp.int32, (N_GRP, P_DEV, N_HH, N_HH), 2)
    source = lax.broadcasted_iota(jnp.int32, (N_GRP, P_DEV, N_HH, N_HH), 3)
    return jnp.where(owner == source, CAP, filled).astype(jnp.int32)


def with_ends(values, own_key, smallest, top_value):
    shape = values.shape
    index_at = [jax.random.randint(jax.random.fold_in(own_key, axis), (), 0, shape[axis]) for axis in range(len(shape))]
    values = values.at[tuple(index_at)].set(smallest)
    longest = shape.index(max(shape))
    index_at[longest] = (index_at[longest] + 1) % shape[longest]
    return values.at[tuple(index_at)].set(top_value)


def level_of(rng, dims, cuts, low, high):
    def one(dim, shards_of):
        heights = jax.random.uniform(jax.random.fold_in(jax.random.fold_in(rng, 6), dim), (shards_of,), jnp.float32, low / len(cuts), high / len(cuts))
        return jnp.repeat(jnp.exp(heights), dims[dim] // shards_of).reshape((-1,) + (1,) * (len(dims) - dim - 1))

    level = one(*cuts[0])
    for cut in cuts[1:]:
        level = level * one(*cut)
    return level


def bell_draw(own_key, dims, deviation, reach, shards=(), held_as=jnp.bfloat16):
    values = deviation * jax.random.normal(own_key, dims, jnp.float32)
    if shards:
        values = values * level_of(own_key, dims, shards, -0.22, 0.18)
    return jnp.clip(values, -reach, reach).astype(held_as)


def setup_inputs(seed: int = 0) -> dict:
    key_list = jax.random.split(jax.random.key(seed), 6)
    hh_factors = draw_hh_factors(jax.random.fold_in(key_list[5], 71), 0)
    prod_init = bell_draw(key_list[1], (P_SIZE, K), 0.2, 1.2, ((0, 32),), jnp.float32)
    hh_index = with_ends(jax.random.randint(key_list[2], (N_GRP, P_DEV, N_HH, N_HH, CAP), 0, HH_DEV), jax.random.fold_in(key_list[2], 1), 0, HH_DEV - 1).astype(jnp.int32)
    trips = with_ends(jax.random.randint(key_list[3], (N_GRP, P_DEV, N_HH, N_HH, CAP), 1, 9), jax.random.fold_in(key_list[3], 1), 1, 8).astype(jnp.int32)
    counts = draw_counts(jax.random.fold_in(key_list[5], 71), 0)
    return {"hh_factors": hh_factors, "prod_init": prod_init, "hh_index": hh_index, "trips": trips, "counts": counts}


conf_scale = 40.0
ridge_term = 16.0
small_eps = 1e-6


def apply_matrix(gram, factors, weighted, vector):
    dense = jnp.dot(vector, gram, precision=lax.Precision.HIGHEST)
    inner = jnp.einsum('plm,pm->pl', weighted.astype(jnp.float32), vector, precision=lax.Precision.HIGHEST)
    spread = jnp.einsum('plk,pl->pk', factors.astype(jnp.float32), inner, precision=lax.Precision.HIGHEST)
    return dense + spread + ridge_term * vector


def solve_block(gram, factors, weighted, coef, start):
    rhs = jnp.einsum('pl,plk->pk', coef, factors, preferred_element_type=jnp.float32)
    solution = start
    resid = rhs - apply_matrix(gram, factors, weighted, solution)
    direc = resid
    norm_now = jnp.sum(resid * resid, axis=-1)
    for turn_idx in range(2):
        image = apply_matrix(gram, factors, weighted, direc)
        alpha = norm_now / (jnp.sum(direc * image, axis=-1) + small_eps)
        solution = solution + alpha[:, None] * direc
        resid = resid - alpha[:, None] * image
        norm_next = jnp.sum(resid * resid, axis=-1)
        direc = resid + (norm_next / (norm_now + small_eps))[:, None] * direc
        norm_now = norm_next
    return solution


def reference(hh_factors, prod_init, hh_index, trips, counts):
    gram = lax.dot_general(hh_factors, hh_factors, (((0,), (0,)), ((), ())), preferred_element_type=jnp.float32)
    blocks = N_GRP * N_HH
    index_blk = jnp.transpose(hh_index, (0, 2, 1, 3, 4)).reshape(blocks, P_DEV, N_HH, CAP)
    trips_blk = jnp.transpose(trips, (0, 2, 1, 3, 4)).reshape(blocks, P_DEV, N_HH, CAP)
    counts_blk = jnp.transpose(counts, (0, 2, 1, 3)).reshape(blocks, P_DEV, N_HH)
    init_blk = prod_init.reshape(blocks, P_DEV, K)

    def one_block(pieces):
        index_one, trips_one, counts_one, start = pieces
        source = lax.broadcasted_iota(jnp.int32, index_one.shape, 1)
        global_ids = (source * HH_DEV + index_one).astype(jnp.int32)
        factors = jnp.take(hh_factors, global_ids.reshape(-1), axis=0).reshape(P_DEV, N_HH * CAP, K)
        slot = lax.broadcasted_iota(jnp.int32, index_one.shape, 2)
        live = (slot < counts_one[:, :, None]).astype(jnp.float32).reshape(P_DEV, N_HH * CAP)
        weight = conf_scale * jnp.log1p(trips_one.astype(jnp.float32)).reshape(P_DEV, N_HH * CAP) * live
        weighted = (weight[:, :, None] * factors.astype(jnp.float32)).astype(jnp.bfloat16)
        coef = (live * (1.0 + weight)).astype(jnp.bfloat16)
        return solve_block(gram, factors, weighted, coef, start)

    result = lax.map(one_block, (index_blk, trips_blk, counts_blk, init_blk))
    return result.reshape(P_SIZE, K)
```

```python
import functools

import jax
import jax.numpy as jnp
from jax import lax
from jax.experimental import pallas as pl
from jax.experimental.pallas import tpu as pltpu
from jax.sharding import PartitionSpec as P

conf_scale = 40.0
ridge_term = 16.0
small_eps = 1e-06
half_word = 16

NN = (((1,), (0,)), ((), ()))
NT = (((1,), (1,)), ((), ()))


def dot(left, right, dims=NN):
    return lax.dot_general(left, right, dims, preferred_element_type=jnp.float32)


def halves(value):
    high = value.astype(jnp.bfloat16)
    low = (value - high.astype(jnp.float32)).astype(jnp.bfloat16)
    return high, low


def stacked(value):
    return jnp.concatenate(halves(value), axis=0)


def folded(value):
    rows = value.shape[0] // 2
    return value[:rows] + value[rows:]


def solve(code_ref, start_ref, table_ref, out_ref, gram_high, gram_low, rows_ref, weighted_ref, coef_ref):
    sources, width, households = table_ref.shape
    groups = rows_ref.shape[0]
    block = start_ref.shape[0]
    per_group = block // groups
    lanes = code_ref.shape[1] // groups
    cap = lanes // per_group

    @pl.when(pl.program_id(0) == 0)
    def _():
        gram = dot(table_ref[0], table_ref[0], NT)
        for source in range(1, sources):
            gram = gram + dot(table_ref[source], table_ref[source], NT)
        gram_high[...], gram_low[...] = halves(gram)

    household_ids = lax.broadcasted_iota(jnp.int32, (households, lanes), 0)

    def gather(source):
        table = table_ref[source]
        for group in range(groups):
            code = code_ref[pl.ds(source, 1), group * lanes : (group + 1) * lanes]
            trips = code >> half_word
            index = code & ((1 << half_word) - 1)
            weight = conf_scale * jnp.log1p(trips.astype(jnp.float32))
            live = (trips > 0).astype(jnp.float32)
            onehot = (household_ids == index).astype(jnp.float32).astype(jnp.bfloat16)
            picked = dot(table, onehot)
            place = pl.ds(pl.multiple_of(source * lanes, 128), lanes)
            rows_ref[group, :, place] = picked.astype(jnp.bfloat16)
            weighted_ref[group, :, place] = (weight * picked).astype(jnp.bfloat16)
            coef_ref[group, :, place] = (live * (1.0 + weight)).astype(jnp.bfloat16).astype(jnp.float32)

    pl.loop(0, sources)(gather)

    slots = sources * lanes
    row_ids = lax.broadcasted_iota(jnp.int32, (per_group, slots), 0)
    lane_ids = lax.broadcasted_iota(jnp.int32, (per_group, slots), 1)
    own = lax.rem(lane_ids, lanes) // cap == row_ids

    def spread(vector, from_coef):
        pieces = []
        for group in range(groups):
            part = vector[group * per_group : (group + 1) * per_group]
            inner = folded(dot(stacked(part), weighted_ref[group]))
            if from_coef:
                inner = coef_ref[group] - inner
            inner = jnp.where(own, inner, 0.0)
            pieces.append(folded(dot(stacked(inner), rows_ref[group], NT)))
        return jnp.concatenate(pieces, axis=0)

    def dense(vector):
        both = stacked(vector)
        return (
            folded(dot(both, gram_high[...]))
            + dot(both[: vector.shape[0]], gram_low[...])
            + ridge_term * vector
        )

    answer = start_ref[...]
    resid = spread(answer, True) - dense(answer)
    direc = resid
    norm_now = jnp.sum(resid * resid, axis=-1, keepdims=True)
    for turn in range(2):
        image = dense(direc) + spread(direc, False)
        alpha = norm_now / (jnp.sum(direc * image, axis=-1, keepdims=True) + small_eps)
        answer = answer + alpha * direc
        if turn == 0:
            resid = resid - alpha * image
            norm_next = jnp.sum(resid * resid, axis=-1, keepdims=True)
            direc = resid + (norm_next / (norm_now + small_eps)) * direc
            norm_now = norm_next
    out_ref[...] = answer


def shards(hh_factors, prod_init, hh_index, trips, counts):
    households, width = hh_factors.shape
    products = prod_init.shape[0]
    sources = lax.axis_size("hh")
    cap = hh_index.shape[4]
    table = lax.all_gather(hh_factors.T, "hh", axis=0)
    slot_ids = lax.broadcasted_iota(jnp.int32, hh_index.shape, 4)
    live_trips = jnp.where(slot_ids < counts[..., None], trips, 0)
    code = (live_trips << half_word) | hh_index
    code = code.reshape(products, sources, cap).transpose(1, 0, 2).reshape(sources, products * cap)
    code = lax.all_to_all(code, "hh", split_axis=0, concat_axis=0, tiled=True)

    per_group = 64 if products % 64 == 0 else products
    block = products if products * sources * cap <= 16384 else per_group
    groups = block // per_group
    lanes = per_group * cap
    return pl.pallas_call(
        solve,
        grid=(products // block,),
        out_shape=jax.ShapeDtypeStruct(prod_init.shape, jnp.float32),
        in_specs=[
            pl.BlockSpec((sources, block * cap), lambda i: (0, i)),
            pl.BlockSpec((block, width), lambda i: (i, 0)),
            pl.BlockSpec(memory_space=pltpu.VMEM),
        ],
        out_specs=pl.BlockSpec((block, width), lambda i: (i, 0)),
        scratch_shapes=[
            pltpu.VMEM((width, width), jnp.bfloat16),
            pltpu.VMEM((width, width), jnp.bfloat16),
            pltpu.VMEM((groups, width, sources * lanes), jnp.bfloat16),
            pltpu.VMEM((groups, width, sources * lanes), jnp.bfloat16),
            pltpu.VMEM((groups, 1, sources * lanes), jnp.float32),
        ],
        compiler_params=pltpu.CompilerParams(vmem_limit_bytes=60 * 2**20),
    )(code, prod_init, table)


def solution(mesh):
    placed = (
        P("hh", None),
        P(("grp", "hh"), None),
        P("grp", None, None, "hh", None),
        P("grp", None, None, "hh", None),
        P("grp", None, None, "hh"),
    )
    return jax.shard_map(
        shards, mesh=mesh, in_specs=placed, out_specs=P(("grp", "hh"), None), check_vma=False
    )
```

```python
import functools

import jax
import jax.numpy as jnp
from jax import lax
from jax.experimental import pallas as pl
from jax.experimental.pallas import tpu as pltpu
from jax.sharding import PartitionSpec as P

conf_scale = 40.0
ridge_term = 16.0
small_eps = 1e-06
half_word = 16

NN = (((1,), (0,)), ((), ()))
NT = (((1,), (1,)), ((), ()))


def dot(left, right, dims=NN):
    return lax.dot_general(left, right, dims, preferred_element_type=jnp.float32)


def halves(value):
    high = value.astype(jnp.bfloat16)
    low = (value - high.astype(jnp.float32)).astype(jnp.bfloat16)
    return high, low


def stacked(value):
    return jnp.concatenate(halves(value), axis=0)


def folded(value):
    rows = value.shape[0] // 2
    return value[:rows] + value[rows:]


def gather(table, code, household_ids):
    trips = code >> half_word
    index = code & ((1 << half_word) - 1)
    weight = conf_scale * jnp.log1p(trips.astype(jnp.float32))
    live = (trips > 0).astype(jnp.float32)
    picked = None
    for quarter, piece in enumerate(table):
        ids = household_ids + quarter * household_ids.shape[0]
        onehot = (ids == index).astype(jnp.float32).astype(jnp.bfloat16)
        part = dot(piece, onehot)
        picked = part if picked is None else picked + part
    coef = (live * (1.0 + weight)).astype(jnp.bfloat16).astype(jnp.float32)
    return picked.astype(jnp.bfloat16), (weight * picked).astype(jnp.bfloat16), coef


def conjugate(start, gram_high, gram_low, rows_ref, weighted_ref, coef_ref, cap):
    groups, _, slots = rows_ref.shape
    per_group = start.shape[0] // groups
    lanes = per_group * cap
    row_ids = lax.broadcasted_iota(jnp.int32, (per_group, slots), 0)
    lane_ids = lax.broadcasted_iota(jnp.int32, (per_group, slots), 1)
    own = lax.rem(lane_ids, lanes) // cap == row_ids

    def spread(vector, from_coef):
        pieces = []
        for group in range(groups):
            part = vector[group * per_group : (group + 1) * per_group]
            inner = folded(dot(stacked(part), weighted_ref[group]))
            if from_coef:
                inner = coef_ref[group] - inner
            inner = jnp.where(own, inner, 0.0)
            pieces.append(folded(dot(stacked(inner), rows_ref[group], NT)))
        return jnp.concatenate(pieces, axis=0)

    def dense(vector):
        both = stacked(vector)
        return (
            folded(dot(both, gram_high))
            + dot(both[: vector.shape[0]], gram_low)
            + ridge_term * vector
        )

    answer = start
    resid = spread(answer, True) - dense(answer)
    direc = resid
    norm_now = jnp.sum(resid * resid, axis=-1, keepdims=True)
    for turn in range(2):
        image = dense(direc) + spread(direc, False)
        alpha = norm_now / (jnp.sum(direc * image, axis=-1, keepdims=True) + small_eps)
        answer = answer + alpha * direc
        if turn == 0:
            resid = resid - alpha * image
            norm_next = jnp.sum(resid * resid, axis=-1, keepdims=True)
            direc = resid + (norm_next / (norm_now + small_eps)) * direc
            norm_now = norm_next
    return answer


def solve_blocks(code_ref, start_ref, table_ref, out_ref, gram_high, gram_low, rows_ref, weighted_ref, coef_ref):
    sources, width, households = table_ref.shape
    groups = rows_ref.shape[0]
    lanes = code_ref.shape[1] // groups

    @pl.when(pl.program_id(0) == 0)
    def _():
        gram = dot(table_ref[0], table_ref[0], NT)
        for source in range(1, sources):
            gram = gram + dot(table_ref[source], table_ref[source], NT)
        gram_high[...], gram_low[...] = halves(gram)

    household_ids = lax.broadcasted_iota(jnp.int32, (households, lanes), 0)

    def fill(source):
        for group in range(groups):
            code = code_ref[pl.ds(source, 1), group * lanes : (group + 1) * lanes]
            place = pl.ds(pl.multiple_of(source * lanes, 128), lanes)
            rows, weighted, coef = gather([table_ref[source]], code, household_ids)
            rows_ref[group, :, place] = rows
            weighted_ref[group, :, place] = weighted
            coef_ref[group, :, place] = coef

    pl.loop(0, sources)(fill)
    cap = lanes * groups // start_ref.shape[0]
    out_ref[...] = conjugate(
        start_ref[...], gram_high[...], gram_low[...], rows_ref, weighted_ref, coef_ref, cap
    )


def exchange_and_solve(
    n_grp, n_hh, cores, code_ref, start_ref, shard_ref, out_ref, table, codes, gram_ref,
    rows_ref, weighted_ref, coef_ref, code_sems, shard_sems, line_sems, plane_sems, core_sems,
):
    grp, hh = lax.axis_index("grp"), lax.axis_index("hh")
    n_line = n_hh // cores
    line, core = hh // cores, lax.rem(hh, cores)
    twin = line * cores + lax.rem(core + 1, cores)
    _, quarters, width, piece_rows = table.shape
    groups = rows_ref.shape[0]
    lanes = code_ref.shape[2] // groups

    def remote(source, target, sems, place, device):
        return pltpu.make_async_remote_copy(
            src_ref=source,
            dst_ref=target,
            send_sem=sems.at[(0,) + place],
            recv_sem=sems.at[(1,) + place],
            device_id=device,
            device_id_type=pl.DeviceIdType.MESH,
        )

    barrier = pltpu.get_barrier_semaphore()
    for step in range(1, n_hh):
        pl.semaphore_signal(
            barrier, inc=1, device_id=(grp, lax.rem(hh + step, n_hh)), device_id_type=pl.DeviceIdType.MESH
        )
    for step in range(1, n_grp):
        pl.semaphore_signal(
            barrier, inc=1, device_id=(lax.rem(grp + step, n_grp), hh), device_id_type=pl.DeviceIdType.MESH
        )
    pl.semaphore_wait(barrier, n_hh + n_grp - 2)

    sent = []

    def send(copy):
        copy.start()
        sent.append(copy)

    def line_peer(step):
        return lax.rem(line + step, n_line) * cores + core

    def line_source(step, at_core):
        return lax.rem(line + n_line - step, n_line) * cores + at_core

    def plane_source(step):
        return lax.rem(grp + n_grp - step, n_grp)

    for step in range(1, n_line):
        send(remote(shard_ref.at[grp], table.at[hh, grp], line_sems, (step - 1,), (grp, line_peer(step))))
    send(remote(shard_ref, table.at[hh], shard_sems, (0,), (grp, twin)))
    for step in range(1, n_hh):
        target = lax.rem(hh + step, n_hh)
        send(remote(code_ref.at[target], codes.at[hh], code_sems, (step - 1,), (grp, target)))

    household_ids = lax.broadcasted_iota(jnp.int32, (piece_rows, lanes), 0)

    def fill(source, shard, code, first=False):
        gram = dot(shard[0], shard[0], NT)
        for quarter in range(1, quarters):
            gram = gram + dot(shard[quarter], shard[quarter], NT)
        if first:
            gram_ref[...] = gram
        else:
            gram_ref[...] += gram
        place = pl.ds(pl.multiple_of(source * lanes, 128), lanes)

        def fill_group(group):
            here = code[:, pl.ds(pl.multiple_of(group * lanes, 128), lanes)]
            rows, weighted, coef = gather([shard[q] for q in range(quarters)], here, household_ids)
            rows_ref[group, :, place] = rows
            weighted_ref[group, :, place] = weighted
            coef_ref[group, :, place] = coef

        pl.loop(0, groups)(fill_group)

    fill(hh, shard_ref, code_ref.at[hh], True)

    def forward_core(step, slot, quarter):
        piece = table.at[line_source(step, core), quarter]
        send(remote(piece, piece, core_sems, (step - 1, slot), (grp, twin)))

    for step in range(1, n_line):
        piece = table.at[line_source(step, core), grp]
        remote(piece, piece, line_sems, (step - 1,), (grp, hh)).wait_recv()
        for hop in range(1, n_grp):
            device = (lax.rem(grp + hop, n_grp), hh)
            send(remote(piece, piece, plane_sems, (step - 1, hop - 1), device))
        forward_core(step, 0, grp)

    for step in range(1, n_hh):
        target = lax.rem(hh + n_hh - step, n_hh)
        remote(codes.at[target], codes.at[target], code_sems, (step - 1,), (grp, hh)).wait_recv()

    remote(table.at[twin], table.at[twin], shard_sems, (0,), (grp, hh)).wait_recv()
    fill(twin, table.at[twin], codes.at[twin])

    def fill_twin(step):
        source = line_source(step, lax.rem(core + 1, cores))
        for slot in range(n_grp):
            piece = table.at[source, plane_source(slot)]
            remote(piece, piece, core_sems, (step - 1, slot), (grp, hh)).wait_recv()
        fill(source, table.at[source], codes.at[source])

    for step in range(1, n_line):
        source = line_source(step, core)
        for hop in range(1, n_grp):
            piece = table.at[source, plane_source(hop)]
            remote(piece, piece, plane_sems, (step - 1, hop - 1), (grp, hh)).wait_recv()
            forward_core(step, hop, plane_source(hop))
        if step > 1:
            fill_twin(step - 1)
        fill(source, table.at[source], codes.at[source])
    fill_twin(n_line - 1)

    gram_high, gram_low = halves(gram_ref[...])
    cap = lanes * groups // start_ref.shape[0]
    out_ref[...] = conjugate(
        start_ref[...], gram_high, gram_low, rows_ref, weighted_ref, coef_ref, cap
    )
    for copy in sent:
        copy.wait_send()


def shards(hh_factors, prod_init, hh_index, trips, counts):
    households, width = hh_factors.shape
    products = prod_init.shape[0]
    sources = lax.axis_size("hh")
    cap = hh_index.shape[4]
    slot_ids = lax.broadcasted_iota(jnp.int32, hh_index.shape, 4)
    live_trips = jnp.where(slot_ids < counts[..., None], trips, 0)
    code = (live_trips << half_word) | hh_index
    code = code.reshape(products, sources, cap).transpose(1, 0, 2).reshape(sources, products * cap)
    cores = 2
    n_grp = lax.axis_size("grp")
    per_group = 64 if products % 64 == 0 else products
    lanes = per_group * cap
    fits = products * sources * cap <= 16384 and sources % cores == 0
    block = products if fits else per_group
    groups = block // per_group
    wide = (groups, width, sources * lanes)
    gathered = [
        pltpu.VMEM(wide, jnp.bfloat16),
        pltpu.VMEM(wide, jnp.bfloat16),
        pltpu.VMEM((groups, 1, sources * lanes), jnp.float32),
    ]
    answer_shape = jax.ShapeDtypeStruct(prod_init.shape, jnp.float32)
    if fits:
        piece_rows = households // n_grp
        shard = hh_factors.reshape(n_grp, piece_rows, width).transpose(0, 2, 1)
        n_line = sources // cores
        dma = pltpu.SemaphoreType.DMA
        return pl.pallas_call(
            functools.partial(exchange_and_solve, n_grp, sources, cores),
            out_shape=answer_shape,
            in_specs=[pl.BlockSpec(memory_space=pltpu.VMEM)] * 3,
            out_specs=pl.BlockSpec(memory_space=pltpu.VMEM),
            scratch_shapes=[
                pltpu.VMEM((sources, n_grp, width, piece_rows), jnp.bfloat16),
                pltpu.VMEM((sources, 1, products * cap), jnp.int32),
                pltpu.VMEM((width, width), jnp.float32),
                *gathered,
                dma((2, sources - 1)),
                dma((2, 1)),
                dma((2, n_line - 1)),
                dma((2, n_line - 1, n_grp - 1)),
                dma((2, n_line - 1, n_grp)),
            ],
            compiler_params=pltpu.CompilerParams(
                collective_id=0, has_side_effects=True, vmem_limit_bytes=60 * 2**20
            ),
        )(code.reshape(sources, 1, products * cap), prod_init, shard)

    table = lax.all_gather(hh_factors.T, "hh", axis=0)
    code = lax.all_to_all(code, "hh", split_axis=0, concat_axis=0, tiled=True)
    return pl.pallas_call(
        solve_blocks,
        grid=(products // block,),
        out_shape=answer_shape,
        in_specs=[
            pl.BlockSpec((sources, block * cap), lambda i: (0, i)),
            pl.BlockSpec((block, width), lambda i: (i, 0)),
            pl.BlockSpec(memory_space=pltpu.VMEM),
        ],
        out_specs=pl.BlockSpec((block, width), lambda i: (i, 0)),
        scratch_shapes=[
            pltpu.VMEM((width, width), jnp.bfloat16),
            pltpu.VMEM((width, width), jnp.bfloat16),
            *gathered,
        ],
        compiler_params=pltpu.CompilerParams(vmem_limit_bytes=60 * 2**20),
    )(code, prod_init, table)


def solution(mesh):
    placed = (
        P("hh", None),
        P(("grp", "hh"), None),
        P("grp", None, None, "hh", None),
        P("grp", None, None, "hh", None),
        P("grp", None, None, "hh"),
    )
    return jax.shard_map(
        shards, mesh=mesh, in_specs=placed, out_specs=P(("grp", "hh"), None), check_vma=False
    )
```

```python
import functools

import jax
import jax.numpy as jnp
from jax import lax
from jax.experimental import pallas as pl
from jax.experimental.pallas import tpu as pltpu
from jax.sharding import PartitionSpec as P

conf_scale = 40.0
ridge_term = 16.0
small_eps = 1e-06
half_word = 16

NN = (((1,), (0,)), ((), ()))
NT = (((1,), (1,)), ((), ()))


def dot(left, right, dims=NN):
    return lax.dot_general(left, right, dims, preferred_element_type=jnp.float32)


def halves(value):
    high = value.astype(jnp.bfloat16)
    low = (value - high.astype(jnp.float32)).astype(jnp.bfloat16)
    return high, low


def stacked(value):
    return jnp.concatenate(halves(value), axis=0)


def folded(value):
    rows = value.shape[0] // 2
    return value[:rows] + value[rows:]


def gather(table, code, household_ids):
    trips = code >> half_word
    index = code & ((1 << half_word) - 1)
    weight = conf_scale * jnp.log1p(trips.astype(jnp.float32))
    live = (trips > 0).astype(jnp.float32)
    picked = None
    for quarter, piece in enumerate(table):
        ids = household_ids + quarter * household_ids.shape[0]
        onehot = (ids == index).astype(jnp.float32).astype(jnp.bfloat16)
        part = dot(piece, onehot)
        picked = part if picked is None else picked + part
    coef = (live * (1.0 + weight)).astype(jnp.bfloat16).astype(jnp.float32)
    return picked.T.astype(jnp.bfloat16), (weight * picked).astype(jnp.bfloat16), coef


def conjugate(start, gram_high, gram_low, rows_ref, weighted_ref, coef_ref, cap):
    groups, slots, _ = rows_ref.shape
    per_group = start.shape[0] // groups
    lanes = per_group * cap
    row_ids = lax.broadcasted_iota(jnp.int32, (per_group, lanes), 0)
    lane_ids = lax.broadcasted_iota(jnp.int32, (per_group, lanes), 1)
    first = row_ids * cap
    inside = jnp.logical_and(lane_ids >= first, lane_ids < first + cap)
    own = jnp.concatenate([inside.astype(jnp.float32)] * (slots // lanes), axis=1) > 0.0

    def spread(vector, from_coef):
        pieces = []
        for group in range(groups):
            part = vector[group * per_group : (group + 1) * per_group]
            inner = folded(dot(stacked(part), weighted_ref[group]))
            if from_coef:
                inner = coef_ref[group] - inner
            inner = jnp.where(own, inner, 0.0)
            pieces.append(folded(dot(stacked(inner), rows_ref[group])))
        return jnp.concatenate(pieces, axis=0)

    def dense(vector):
        both = stacked(vector)
        return (
            folded(dot(both, gram_high))
            + dot(both[: vector.shape[0]], gram_low)
            + ridge_term * vector
        )

    answer = start
    resid = spread(answer, True) - dense(answer)
    direc = resid
    norm_now = jnp.sum(resid * resid, axis=-1, keepdims=True)
    for turn in range(2):
        image = dense(direc) + spread(direc, False)
        alpha = norm_now / (jnp.sum(direc * image, axis=-1, keepdims=True) + small_eps)
        answer = answer + alpha * direc
        if turn == 0:
            resid = resid - alpha * image
            norm_next = jnp.sum(resid * resid, axis=-1, keepdims=True)
            direc = resid + (norm_next / (norm_now + small_eps)) * direc
            norm_now = norm_next
    return answer


def solve_blocks(code_ref, start_ref, table_ref, out_ref, gram_high, gram_low, rows_ref, weighted_ref, coef_ref):
    sources, width, households = table_ref.shape
    groups = rows_ref.shape[0]
    lanes = code_ref.shape[1] // groups

    @pl.when(pl.program_id(0) == 0)
    def _():
        gram = dot(table_ref[0], table_ref[0], NT)
        for source in range(1, sources):
            gram = gram + dot(table_ref[source], table_ref[source], NT)
        gram_high[...], gram_low[...] = halves(gram)

    household_ids = lax.broadcasted_iota(jnp.int32, (households, lanes), 0)

    def fill(source):
        for group in range(groups):
            code = code_ref[pl.ds(source, 1), group * lanes : (group + 1) * lanes]
            place = pl.ds(pl.multiple_of(source * lanes, 128), lanes)
            rows, weighted, coef = gather([table_ref[source]], code, household_ids)
            rows_ref[group, place, :] = rows
            weighted_ref[group, :, place] = weighted
            coef_ref[group, :, place] = coef

    pl.loop(0, sources)(fill)
    cap = lanes * groups // start_ref.shape[0]
    out_ref[...] = conjugate(
        start_ref[...], gram_high[...], gram_low[...], rows_ref, weighted_ref, coef_ref, cap
    )


def exchange_and_solve(
    n_grp, n_hh, cores, code_ref, start_ref, shard_ref, out_ref, table, codes, gram_ref,
    rows_ref, weighted_ref, coef_ref, code_sems, shard_sems, line_sems, plane_sems, core_sems,
):
    grp, hh = lax.axis_index("grp"), lax.axis_index("hh")
    n_line = n_hh // cores
    line, core = hh // cores, lax.rem(hh, cores)
    twin = line * cores + lax.rem(core + 1, cores)
    _, quarters, width, piece_rows = table.shape
    groups = rows_ref.shape[0]
    lanes = code_ref.shape[2] // groups

    def remote(source, target, sems, place, device):
        return pltpu.make_async_remote_copy(
            src_ref=source,
            dst_ref=target,
            send_sem=sems.at[(0,) + place],
            recv_sem=sems.at[(1,) + place],
            device_id=device,
            device_id_type=pl.DeviceIdType.MESH,
        )

    barrier = pltpu.get_barrier_semaphore()
    for step in range(1, n_hh):
        pl.semaphore_signal(
            barrier, inc=1, device_id=(grp, lax.rem(hh + step, n_hh)), device_id_type=pl.DeviceIdType.MESH
        )
    for step in range(1, n_grp):
        pl.semaphore_signal(
            barrier, inc=1, device_id=(lax.rem(grp + step, n_grp), hh), device_id_type=pl.DeviceIdType.MESH
        )
    pl.semaphore_wait(barrier, n_hh + n_grp - 2)

    sent = []

    def send(copy):
        copy.start()
        sent.append(copy)

    def line_peer(step):
        return lax.rem(line + step, n_line) * cores + core

    def line_source(step, at_core):
        return lax.rem(line + n_line - step, n_line) * cores + at_core

    def plane_source(step):
        return lax.rem(grp + n_grp - step, n_grp)

    for step in range(1, n_line):
        send(remote(shard_ref.at[grp], table.at[hh, grp], line_sems, (step - 1,), (grp, line_peer(step))))
    send(remote(shard_ref, table.at[hh], shard_sems, (0,), (grp, twin)))
    for step in range(1, n_hh):
        target = lax.rem(hh + step, n_hh)
        send(remote(code_ref.at[target], codes.at[hh], code_sems, (step - 1,), (grp, target)))

    household_ids = lax.broadcasted_iota(jnp.int32, (piece_rows, lanes), 0)

    def fill(source, shard, code, first=False):
        gram = dot(shard[0], shard[0], NT)
        for quarter in range(1, quarters):
            gram = gram + dot(shard[quarter], shard[quarter], NT)
        if first:
            gram_ref[...] = gram
        else:
            gram_ref[...] += gram
        place = pl.ds(pl.multiple_of(source * lanes, 128), lanes)

        def fill_group(group):
            here = code[:, pl.ds(pl.multiple_of(group * lanes, 128), lanes)]
            rows, weighted, coef = gather([shard[q] for q in range(quarters)], here, household_ids)
            rows_ref[group, place, :] = rows
            weighted_ref[group, :, place] = weighted
            coef_ref[group, :, place] = coef

        pl.loop(0, groups)(fill_group)

    fill(hh, shard_ref, code_ref.at[hh], True)

    def forward_core(step, slot, quarter):
        piece = table.at[line_source(step, core), quarter]
        send(remote(piece, piece, core_sems, (step - 1, slot), (grp, twin)))

    for step in range(1, n_line):
        piece = table.at[line_source(step, core), grp]
        remote(piece, piece, line_sems, (step - 1,), (grp, hh)).wait_recv()
        for hop in range(1, n_grp):
            device = (lax.rem(grp + hop, n_grp), hh)
            send(remote(piece, piece, plane_sems, (step - 1, hop - 1), device))
        forward_core(step, 0, grp)

    for step in range(1, n_hh):
        target = lax.rem(hh + n_hh - step, n_hh)
        remote(codes.at[target], codes.at[target], code_sems, (step - 1,), (grp, hh)).wait_recv()

    remote(table.at[twin], table.at[twin], shard_sems, (0,), (grp, hh)).wait_recv()
    fill(twin, table.at[twin], codes.at[twin])

    def fill_twin(step):
        source = line_source(step, lax.rem(core + 1, cores))
        for slot in range(n_grp):
            piece = table.at[source, plane_source(slot)]
            remote(piece, piece, core_sems, (step - 1, slot), (grp, hh)).wait_recv()
        fill(source, table.at[source], codes.at[source])

    for step in range(1, n_line):
        source = line_source(step, core)
        for hop in range(1, n_grp):
            piece = table.at[source, plane_source(hop)]
            remote(piece, piece, plane_sems, (step - 1, hop - 1), (grp, hh)).wait_recv()
            forward_core(step, hop, plane_source(hop))
        if step > 1:
            fill_twin(step - 1)
        fill(source, table.at[source], codes.at[source])
    fill_twin(n_line - 1)

    gram_high, gram_low = halves(gram_ref[...])
    cap = lanes * groups // start_ref.shape[0]
    out_ref[...] = conjugate(
        start_ref[...], gram_high, gram_low, rows_ref, weighted_ref, coef_ref, cap
    )
    for copy in sent:
        copy.wait_send()


def shards(hh_factors, prod_init, hh_index, trips, counts):
    households, width = hh_factors.shape
    products = prod_init.shape[0]
    sources = lax.axis_size("hh")
    cap = hh_index.shape[4]
    slot_ids = lax.broadcasted_iota(jnp.int32, hh_index.shape, 4)
    live_trips = jnp.where(slot_ids < counts[..., None], trips, 0)
    code = (live_trips << half_word) | hh_index
    code = code.reshape(products, sources, cap).transpose(1, 0, 2).reshape(sources, products * cap)
    cores = 2
    n_grp = lax.axis_size("grp")
    per_group = 64 if products % 64 == 0 else products
    lanes = per_group * cap
    fits = products * sources * cap <= 16384 and sources % cores == 0
    block = products if fits else per_group
    groups = block // per_group
    wide = (groups, width, sources * lanes)
    gathered = [
        pltpu.VMEM((groups, sources * lanes, width), jnp.bfloat16),
        pltpu.VMEM(wide, jnp.bfloat16),
        pltpu.VMEM((groups, 1, sources * lanes), jnp.float32),
    ]
    answer_shape = jax.ShapeDtypeStruct(prod_init.shape, jnp.float32)
    if fits:
        piece_rows = households // n_grp
        shard = hh_factors.reshape(n_grp, piece_rows, width).transpose(0, 2, 1)
        n_line = sources // cores
        dma = pltpu.SemaphoreType.DMA
        return pl.pallas_call(
            functools.partial(exchange_and_solve, n_grp, sources, cores),
            out_shape=answer_shape,
            in_specs=[pl.BlockSpec(memory_space=pltpu.VMEM)] * 3,
            out_specs=pl.BlockSpec(memory_space=pltpu.VMEM),
            scratch_shapes=[
                pltpu.VMEM((sources, n_grp, width, piece_rows), jnp.bfloat16),
                pltpu.VMEM((sources, 1, products * cap), jnp.int32),
                pltpu.VMEM((width, width), jnp.float32),
                *gathered,
                dma((2, sources - 1)),
                dma((2, 1)),
                dma((2, n_line - 1)),
                dma((2, n_line - 1, n_grp - 1)),
                dma((2, n_line - 1, n_grp)),
            ],
            compiler_params=pltpu.CompilerParams(
                collective_id=0, has_side_effects=True, vmem_limit_bytes=60 * 2**20
            ),
        )(code.reshape(sources, 1, products * cap), prod_init, shard)

    table = lax.all_gather(hh_factors.T, "hh", axis=0)
    code = lax.all_to_all(code, "hh", split_axis=0, concat_axis=0, tiled=True)
    return pl.pallas_call(
        solve_blocks,
        grid=(products // block,),
        out_shape=answer_shape,
        in_specs=[
            pl.BlockSpec((sources, block * cap), lambda i: (0, i)),
            pl.BlockSpec((block, width), lambda i: (i, 0)),
            pl.BlockSpec(memory_space=pltpu.VMEM),
        ],
        out_specs=pl.BlockSpec((block, width), lambda i: (i, 0)),
        scratch_shapes=[
            pltpu.VMEM((width, width), jnp.bfloat16),
            pltpu.VMEM((width, width), jnp.bfloat16),
            *gathered,
        ],
        compiler_params=pltpu.CompilerParams(vmem_limit_bytes=60 * 2**20),
    )(code, prod_init, table)


def solution(mesh):
    placed = (
        P("hh", None),
        P(("grp", "hh"), None),
        P("grp", None, None, "hh", None),
        P("grp", None, None, "hh", None),
        P("grp", None, None, "hh"),
    )
    return jax.shard_map(
        shards, mesh=mesh, in_specs=placed, out_specs=P(("grp", "hh"), None), check_vma=False
    )
```
